128 devices in a mesh: sub: 32 (over y, z, x_lo), band: 4 (over x_hi, core).
Axes of the slice: x: 4 (x_hi: 2, x_lo: 2; x = x_hi * 2 + x_lo), y: 4, z: 4, core: 2. Of those that a mesh axis runs over, the one named last changes fastest.
Arguments:
- intensity: bfloat16 [4, 16384, 8192], P(None, ('band', 'sub')), may hold values from -6 to 6
- channel_spans: int32 [16384], replicated, may hold values from 1 to 8
Outputs:
- dedispersed: float32 [4, 2048, 8192], P(None, ('band', 'sub'))
- peak_snr: float32 [4, 2048, 8192], P(None, ('band', 'sub'))
The draws below stay inside these ranges and needn't reach their ends.
All inputs are finite; a program needn't handle non-finite values.
Results may differ from the reference program's by a relative error of at most 0.0003.
Values sent between devices are 32-bit elements; how exact they have to be, the bound alone decides.
A program may use at most 128 MiB of HBM per device.

```python
import math
import jax
import jax.numpy as jnp
import numpy as np
from jax import lax

CHAN_DEV = 128
ROWS_DEV = 16
BEAMS = 4
SAMPLES = 8192
BOXES = 9
CH = 16384
DM = 2048
DEVICES = 128


def plant(values, rng, smallest, high):
    longest = values.shape.index(max(values.shape))
    spots = []
    for shift in (0, 1):
        where = [jax.random.randint(jax.random.fold_in(rng, axis), (), 0, length) for axis, length in enumerate(values.shape)]
        where[longest] = (where[longest] + shift) % values.shape[longest]
        spots.append(tuple(where))
    return values.at[spots[0]].set(smallest).at[spots[1]].set(high)


def block_scale(key, shape, cuts, smallest, largest):
    loudness, own = 1.0, jax.random.fold_in(key, 6)
    for axis_at, parts in cuts:
        heights = jnp.exp(jax.random.uniform(jax.random.fold_in(own, axis_at), (parts,), jnp.float32, smallest / len(cuts), largest / len(cuts)))
        loudness = loudness * jnp.repeat(heights, shape[axis_at] // parts).reshape([-1 if axis == axis_at else 1 for axis in range(len(shape))])
    return loudness


def bell_draw(key, shape, deviation, limit, cuts=(), kind=jnp.bfloat16):
    values = deviation * jax.random.normal(key, shape, jnp.float32)
    if cuts:
        values = values * block_scale(key, shape, cuts, -0.22, 0.18)
    return jnp.clip(values, -limit, limit).astype(kind)


def setup_inputs(seed: int = 0) -> dict:
    seeds = jax.random.split(jax.random.key(seed), 3)
    return {
        "intensity": bell_draw(seeds[0], (BEAMS, CH, SAMPLES), 1.0, 6.0, ((1, 128),)),
        "channel_spans": plant(jax.random.randint(seeds[1], (CH,), 1, 9), jax.random.fold_in(seeds[1], 1), 1, 8).astype(jnp.int32),
    }


def reverse_bits(value, bit_total):
    result = 0
    for position in range(bit_total):
        result = result | (value >> position & 1) << bit_total - 1 - position
    return result

def shift_rows(row_data, shifts, margin):
    length = row_data.shape[1]
    padded = jnp.pad(row_data, ((0, 0), (margin, 0)))
    return jax.vmap(lambda one_row, one_shift: lax.dynamic_slice_in_dim(one_row, margin - one_shift, length))(padded, shifts)

def dedisperse_beam(one_beam, channel_spans):
    delay_plane = one_beam.astype(jnp.float32)[:, None, :]
    level_total = CH.bit_length() - 1
    previous_rows = 1
    for tree_level in range(1, level_total + 1):
        row_count = max(1, 2 ** tree_level * ROWS_DEV // CHAN_DEV)
        band_count = CH >> tree_level
        lower_half = delay_plane[0::2]
        upper_half = delay_plane[1::2]
        if row_count > previous_rows:
            lower_half = jnp.repeat(lower_half, row_count // previous_rows, axis=1)
            upper_half = jnp.repeat(upper_half, row_count // previous_rows, axis=1)
        grouped = channel_spans.reshape(band_count, 2, 2 ** (tree_level - 1)).sum(axis=2).astype(jnp.int32)
        row_index = jnp.arange(row_count, dtype=jnp.int32)
        shifts = row_index[None, :] * grouped[:, 0:1] // (grouped[:, 0:1] + grouped[:, 1:2])
        shifted = shift_rows(upper_half.reshape(band_count * row_count, SAMPLES), shifts.reshape(-1), row_count)
        delay_plane = lower_half + shifted.reshape(band_count, row_count, SAMPLES)
        previous_rows = row_count
    top_plane = delay_plane[0]
    bit_total = DEVICES.bit_length() - 1
    reversal = np.array([reverse_bits(value, bit_total) for value in range(DEVICES)], dtype=np.int32)
    ordered = top_plane.reshape(DEVICES, ROWS_DEV, SAMPLES)[reversal].reshape(DM, SAMPLES)
    dedispersed = ordered * (1.0 / math.sqrt(CH))
    running = dedispersed
    peak_value = dedispersed
    box_width = 1
    for doubling in range(BOXES - 1):
        running = running + jnp.pad(running, ((0, 0), (box_width, 0)))[:, :SAMPLES]
        box_width = box_width * 2
        peak_value = jnp.maximum(peak_value, running * (1.0 / math.sqrt(box_width)))
    return (dedispersed, peak_value)

def reference(intensity, channel_spans):
    dedispersed, peak_snr = lax.map(lambda one_beam: dedisperse_beam(one_beam, channel_spans), intensity)
    return (dedispersed, peak_snr)
```

```python
import math

import jax
import jax.numpy as jnp
from jax import lax
from jax.experimental import pallas as pl
from jax.experimental.pallas import tpu as pltpu
from jax.sharding import PartitionSpec as P

ROWS = 16
BOXES = 9
BEAMS = 4
LANES = 128
BODY = 64
PAD = 8
PITCH = PAD + BODY
TOP_PAD = 16
TOP_PITCH = TOP_PAD + BODY
COLUMNS = 1024


def rev2(v):
    return v % 2 * 2 + v // 2


def rev3(v):
    return v % 2 * 4 + v // 2 % 2 * 2 + v // 4


def shift_table(spans):
    sub, band = lax.axis_index("sub"), lax.axis_index("band")
    sums = spans.reshape(1024, 16).sum(axis=1)
    device = band * 32 + sub
    local = lax.dynamic_slice_in_dim(sums, device * 8, 8)
    totals = sums.reshape(128, 8).sum(axis=1)
    group = lax.dynamic_slice_in_dim(totals, device // 8 * 8, 8)
    block = rev3(sub % 8)
    own = block * 16 + rev2(sub // 8) * 4 + rev2(band)
    tables = []
    for widths, rows, first in (
        (local, 4, 0), (local, 8, 0), (local, 16, 0),
        (group, 4, 4 * block), (group, 8, 8 * block), (group, 16, 16 * block),
        (totals, 2, 2 * own), (totals, 4, 4 * own), (totals, 8, 8 * own), (totals, 16, 16 * own),
    ):
        grouped = widths.reshape(16 // rows, 2, -1).sum(axis=2)
        low, high = grouped[:, 0:1], grouped[:, 1:2]
        r = first + jnp.arange(rows, dtype=jnp.int32)[None, :]
        tables.append((r * low // (low + high)).reshape(-1))
    return jnp.concatenate(tables)


def kernel(
    table, x_hbm, ded_hbm, peak_hbm,
    xbuf, g, t5, t6, p7, r1, t8, t9, p10, r2, t11, t12, t13, top, ded, peak,
    in_sem, out_sem, send1, recv1, own1, send2, recv2, own2,
):
    sub, band = lax.axis_index("sub"), lax.axis_index("band")
    y, z, x_lo = sub // 8, sub // 2 % 4, sub % 2
    x_hi, core = band // 2, band % 2
    j = sub % 8
    m = band * 4 + y

    peers1 = []
    for dz in (0, 1, 3, 2):
        for dx in range(2):
            if dz or dx:
                to = (z + dz) % 4 * 2 + (x_lo + dx) % 2
                peers1.append((to, {"sub": y * 8 + to, "band": band}))
    peers2 = []
    for dy in (0, 1, 3, 2):
        for dh in range(2):
            for dc in range(2):
                if dy or dh or dc:
                    y_to = (y + dy) % 4
                    band_to = (x_hi + dh) % 2 * 2 + (core + dc) % 2
                    peers2.append((y_to, band_to, {"sub": y_to * 8 + j, "band": band_to}))

    barrier = pltpu.get_barrier_semaphore()
    for peer in peers1:
        pl.semaphore_signal(barrier, inc=1, device_id=peer[-1], device_id_type=pl.DeviceIdType.MESH)
    for peer in peers2:
        pl.semaphore_signal(barrier, inc=1, device_id=peer[-1], device_id_type=pl.DeviceIdType.MESH)

    def fetch(b):
        return pltpu.make_async_copy(x_hbm.at[b], xbuf.at[b], in_sem.at[b])

    for b in range(BEAMS):
        fetch(b).start()

    zeros = jnp.zeros((PAD, LANES), jnp.float32)
    for ref, count in ((g, 8), (t5, 16), (t6, 16), (t8, 16), (t9, 16), (t11, 16), (t12, 16)):
        for row in range(count):
            ref[pl.ds(row * PITCH, PAD), :] = zeros
    for row in range(16):
        t13[pl.ds(row * TOP_PITCH, PAD), :] = zeros
        t13[pl.ds(row * TOP_PITCH + PAD, PAD), :] = zeros

    def clear(b, _):
        for row in range(16):
            r1[b, row // 2, row % 2, 0:PAD, :] = zeros
            r2[b, row, 0:PAD, :] = zeros
        return 0

    lax.fori_loop(0, BEAMS, clear, 0)

    lane = lax.broadcasted_iota(jnp.int32, (BODY, LANES), 1)

    def moved(near, far, amount):
        return pltpu.roll(jnp.where(lane < LANES - amount, near, far), amount, 1)

    def flat(ref):
        def load(row, back):
            return ref[pl.ds(row * PITCH + PAD - back, BODY), :]
        return load

    def flat_store(ref):
        def store(row, value):
            ref[pl.ds(row * PITCH + PAD, BODY), :] = value
        return store

    def small_level(level, rows, load, store, single=False):
        for entry in range(16):
            pair, i = entry // rows, entry % rows
            if single:
                low, high = 2 * pair, 2 * pair + 1
            else:
                low = pair * rows + i // 2
                high = low + rows // 2
            amount = table[(level - 5) * 16 + entry]
            store(entry, load(low, 0) + moved(load(high, 0), load(high, 1), amount))

    def large_level(level, rows, load, store):
        for entry in range(16):
            pair, i = entry // rows, entry % rows
            low = pair * rows + i // 2
            high = low + rows // 2
            shift = table[(level - 5) * 16 + entry]
            whole, amount = shift // LANES, shift % LANES
            store(entry, load(low, 0) + moved(load(high, whole), load(high, whole + 1), amount))

    member = lax.broadcasted_iota(jnp.int32, (16, 128), 0)
    channel = lax.broadcasted_iota(jnp.int32, (16, 128), 1)
    ones = (channel // 16 == member).astype(jnp.float32).astype(jnp.bfloat16)

    def send_one(b, k):
        to, device = peers1[k]
        return pltpu.make_async_remote_copy(
            src_ref=p7.at[b, pl.ds(2 * rev3(to), 2)],
            dst_ref=r1.at[b, j, :, pl.ds(PAD, BODY), :],
            send_sem=send1.at[b, k],
            recv_sem=recv1.at[b, j],
            device_id=device,
            device_id_type=pl.DeviceIdType.MESH,
        )

    def keep_one(b):
        return pltpu.make_async_copy(
            p7.at[b, pl.ds(2 * rev3(j), 2)], r1.at[b, j, :, pl.ds(PAD, BODY), :], own1.at[b]
        )

    def send_two(b, k):
        y_to, band_to, device = peers2[k]
        return pltpu.make_async_remote_copy(
            src_ref=p10.at[b, rev2(y_to) * 4 + rev2(band_to)],
            dst_ref=r2.at[b, m, pl.ds(PAD, BODY), :],
            send_sem=send2.at[b, k],
            recv_sem=recv2.at[b, m],
            device_id=device,
            device_id_type=pl.DeviceIdType.MESH,
        )

    def keep_two(b):
        return pltpu.make_async_copy(
            p10.at[b, rev2(y) * 4 + rev2(band)], r2.at[b, m, pl.ds(PAD, BODY), :], own2.at[b]
        )

    def first(b):
        fetch(b).wait()

        def columns(c, _):
            part = jnp.dot(
                ones, xbuf[b, :, pl.ds(c * COLUMNS, COLUMNS)], preferred_element_type=jnp.float32
            )
            for k in range(COLUMNS // LANES):
                g[pl.ds(PAD + c * (COLUMNS // LANES) + k, 8, stride=PITCH), :] = part[
                    0:8, k * LANES : (k + 1) * LANES
                ]
            return 0

        lax.fori_loop(0, 8192 // COLUMNS, columns, 0)
        small_level(5, 4, flat(g), flat_store(t5), single=True)
        small_level(6, 8, flat(t5), flat_store(t6))

        def keep(row, value):
            p7[b, row] = value

        small_level(7, 16, flat(t6), keep)

    def start_one(b):
        for k in range(len(peers1)):
            send_one(b, k).start()
        keep_one(b).start()

    first(0)
    pl.semaphore_wait(barrier, len(peers1) + len(peers2))
    start_one(0)

    def step_one(b, _):
        first(b)
        start_one(b)
        return 0

    lax.fori_loop(1, BEAMS, step_one, 0)

    def step_two(b, _):
        keep_one(b).wait()
        for to, _ in peers1:
            pltpu.make_async_copy(
                r1.at[b, to, :, pl.ds(PAD, BODY), :], r1.at[b, to, :, pl.ds(PAD, BODY), :], recv1.at[b, to]
            ).wait()

        def load(row, back):
            return r1[b, row // 2, row % 2, PAD - back : PAD - back + BODY, :]

        small_level(8, 4, load, flat_store(t8))
        small_level(9, 8, flat(t8), flat_store(t9))

        def keep(row, value):
            p10[b, row] = value

        small_level(10, 16, flat(t9), keep)
        for k in range(len(peers2)):
            send_two(b, k).start()
        keep_two(b).start()
        return 0

    lax.fori_loop(0, BEAMS, step_two, 0)

    one_lane = lax.broadcasted_iota(jnp.int32, (8, LANES), 1)

    def step_three(b, _):
        keep_two(b).wait()
        for y_to, band_to, _ in peers2:
            n = band_to * 4 + y_to
            pltpu.make_async_copy(
                r2.at[b, n, pl.ds(PAD, BODY), :], r2.at[b, n, pl.ds(PAD, BODY), :], recv2.at[b, n]
            ).wait()
        for entry in range(16):
            pair = entry // 2
            shift = table[6 * 16 + entry]
            whole, amount = shift // LANES, shift % LANES
            back0 = r2[b, 2 * pair + 1, PAD : PAD + BODY, :]
            back1 = r2[b, 2 * pair + 1, PAD - 1 : PAD - 1 + BODY, :]
            back2 = r2[b, 2 * pair + 1, PAD - 2 : PAD - 2 + BODY, :]
            near = jnp.where(whole == 0, back0, back1)
            far = jnp.where(whole == 0, back1, back2)
            t11[pl.ds(entry * PITCH + PAD, BODY), :] = r2[b, 2 * pair, PAD : PAD + BODY, :] + moved(
                near, far, amount
            )
        large_level(12, 4, flat(t11), flat_store(t12))

        def store13(row, value):
            t13[pl.ds(row * TOP_PITCH + TOP_PAD, BODY), :] = value

        def load13(row, back):
            return t13[pl.ds(row * TOP_PITCH + TOP_PAD - back, BODY), :]

        large_level(13, 8, flat(t12), store13)

        def store14(row, value):
            top[pl.ds(row * BODY, BODY), :] = value * (1.0 / 128.0)

        large_level(14, 16, load13, store14)

        blank = jnp.zeros((8, LANES), jnp.float32)
        for half in range(2):

            def boxes(c, before):
                before = list(before)
                for u in range(8):
                    running = top[pl.ds(half * 8 * BODY + c * 8 + u, 8, stride=BODY), :]
                    column = pl.ds(pl.multiple_of((c * 8 + u) * LANES, LANES), LANES)
                    ded[b, half * 8 : half * 8 + 8, column] = running
                    best = running
                    for k in range(BOXES - 1):
                        width = 2**k
                        if width < LANES:
                            late = pltpu.roll(
                                jnp.where(one_lane < LANES - width, running, before[k]), width, 1
                            )
                        else:
                            late = before[k]
                        before[k] = running
                        running = running + late
                        best = jnp.maximum(best, running * (1.0 / math.sqrt(2 * width)))
                    peak[b, half * 8 : half * 8 + 8, column] = best
                return tuple(before)

            lax.fori_loop(0, BODY // 8, boxes, (blank,) * (BOXES - 1))
        pltpu.make_async_copy(ded.at[b], ded_hbm.at[b], out_sem.at[b, 0]).start()
        pltpu.make_async_copy(peak.at[b], peak_hbm.at[b], out_sem.at[b, 1]).start()
        return 0

    lax.fori_loop(0, BEAMS, step_three, 0)

    def finish(b, _):
        pltpu.make_async_copy(ded.at[b], ded_hbm.at[b], out_sem.at[b, 0]).wait()
        pltpu.make_async_copy(peak.at[b], peak_hbm.at[b], out_sem.at[b, 1]).wait()
        for k in range(len(peers1)):
            send_one(b, k).wait_send()
        for k in range(len(peers2)):
            send_two(b, k).wait_send()
        return 0

    lax.fori_loop(0, BEAMS, finish, 0)


def on_device(intensity, channel_spans):
    plane = jax.ShapeDtypeStruct((BEAMS, ROWS, 8192), jnp.float32)
    vmem = lambda *shape: pltpu.VMEM(shape, jnp.float32)
    dma = pltpu.SemaphoreType.DMA
    return pl.pallas_call(
        kernel,
        out_shape=(plane, plane),
        in_specs=[pl.BlockSpec(memory_space=pltpu.SMEM), pl.BlockSpec(memory_space=pl.ANY)],
        out_specs=(pl.BlockSpec(memory_space=pl.ANY), pl.BlockSpec(memory_space=pl.ANY)),
        scratch_shapes=[
            pltpu.VMEM((BEAMS, 128, 8192), jnp.bfloat16),
            vmem(8 * PITCH, LANES),
            vmem(16 * PITCH, LANES),
            vmem(16 * PITCH, LANES),
            vmem(BEAMS, 16, BODY, LANES),
            vmem(BEAMS, 8, 2, PITCH, LANES),
            vmem(16 * PITCH, LANES),
            vmem(16 * PITCH, LANES),
            vmem(BEAMS, 16, BODY, LANES),
            vmem(BEAMS, 16, PITCH, LANES),
            vmem(16 * PITCH, LANES),
            vmem(16 * PITCH, LANES),
            vmem(16 * TOP_PITCH, LANES),
            vmem(16 * BODY, LANES),
            vmem(BEAMS, ROWS, 8192),
            vmem(BEAMS, ROWS, 8192),
            dma((BEAMS,)),
            dma((BEAMS, 2)),
            dma((BEAMS, 7)),
            dma((BEAMS, 8)),
            dma((BEAMS,)),
            dma((BEAMS, 15)),
            dma((BEAMS, 16)),
            dma((BEAMS,)),
        ],
        compiler_params=pltpu.CompilerParams(
            collective_id=0, has_side_effects=True, vmem_limit_bytes=48 * 2**20
        ),
    )(shift_table(channel_spans), intensity)


def solution(mesh):
    return jax.shard_map(
        on_device,
        mesh=mesh,
        in_specs=(P(None, ("band", "sub"), None), P()),
        out_specs=(P(None, ("band", "sub"), None), P(None, ("band", "sub"), None)),
        check_vma=False,
    )
```

```python
import math

import jax
import jax.numpy as jnp
from jax import lax
from jax.experimental import pallas as pl
from jax.experimental.pallas import tpu as pltpu
from jax.sharding import PartitionSpec as P

ROWS = 16
BOXES = 9
BEAMS = 4
LANES = 128
BODY = 64
PAD = 8
PITCH = PAD + BODY
TOP_PAD = 16
TOP_PITCH = TOP_PAD + BODY
COLUMNS = 1024


def rev2(v):
    return v % 2 * 2 + v // 2


def rev3(v):
    return v % 2 * 4 + v // 2 % 2 * 2 + v // 4


def powers(index, first):
    value = jnp.full(index.shape, first, jnp.int32)
    for k in range(1, 7):
        value = jnp.where(index == k, first * 2**k, value)
    return value


def quotient(top, bottom):
    guess = (top.astype(jnp.float32) / bottom.astype(jnp.float32)).astype(jnp.int32)
    left = top - guess * bottom
    return jnp.where(left < 0, guess - 1, jnp.where(left >= bottom, guess + 1, guess))


def fill_tables(spans, out, device, group, block, own):
    spread = spans[...].astype(jnp.float32)
    totals = jnp.sum(spread, axis=1, keepdims=True)
    entry = lax.broadcasted_iota(jnp.int32, (1, LANES), 1)
    level = entry // 16
    near = level < 3
    rows = jnp.where(near, powers(level, 4), powers(level - 3, 2))
    half = powers(level, 1)
    start = jnp.where(near, group, 0) + entry % 16 // rows * 2 * half
    r = rows * jnp.where(near, block, own) + entry % 16 % rows
    place = lax.broadcasted_iota(jnp.int32, (128, LANES), 0) - start
    low = jnp.sum(jnp.where((place >= 0) & (place < half), totals, 0.0), axis=0, keepdims=True)
    both = jnp.sum(jnp.where((place >= 0) & (place < 2 * half), totals, 0.0), axis=0, keepdims=True)
    low, both = low.astype(jnp.int32), jnp.maximum(both.astype(jnp.int32), 1)
    out[0:1, :] = quotient(r * low, both)

    mine = spans[pl.ds(device, 1), :].astype(jnp.float32)
    entry = lax.broadcasted_iota(jnp.int32, (48, 1), 0)
    level = entry // 16
    rows = powers(level, 4)
    half = powers(level, 16)
    start = entry % 16 // rows * 2 * half
    r = entry % 16 % rows
    place = lax.broadcasted_iota(jnp.int32, (48, LANES), 1) - start
    low = jnp.sum(jnp.where((place >= 0) & (place < half), mine, 0.0), axis=1, keepdims=True)
    both = jnp.sum(jnp.where((place >= 0) & (place < 2 * half), mine, 0.0), axis=1, keepdims=True)
    low, both = low.astype(jnp.int32), jnp.maximum(both.astype(jnp.int32), 1)
    shifts = quotient(r * low, both).astype(jnp.float32)
    diagonal = entry == lax.broadcasted_iota(jnp.int32, (48, LANES), 1)
    out[1:2, :] = jnp.sum(jnp.where(diagonal, shifts, 0.0), axis=0, keepdims=True).astype(jnp.int32)


def kernel(
    spans, x_hbm, ded, peak,
    shifts, table, xbuf, g, t5, t6, p7, r1, t8, t9, p10, r2, t11, t12, t13, top,
    table_sem, in_sem, send1, recv1, own1, send2, recv2, own2,
):
    sub, band = lax.axis_index("sub"), lax.axis_index("band")
    y, z, x_lo = sub // 8, sub // 2 % 4, sub % 2
    x_hi, core = band // 2, band % 2
    j = sub % 8
    m = band * 4 + y

    peers1 = []
    for dz in (0, 1, 3, 2):
        for dx in range(2):
            if dz or dx:
                to = (z + dz) % 4 * 2 + (x_lo + dx) % 2
                peers1.append((to, {"sub": y * 8 + to, "band": band}))
    peers2 = []
    for dy in (0, 1, 3, 2):
        for dh in range(2):
            for dc in range(2):
                if dy or dh or dc:
                    y_to = (y + dy) % 4
                    band_to = (x_hi + dh) % 2 * 2 + (core + dc) % 2
                    peers2.append((y_to, band_to, {"sub": y_to * 8 + j, "band": band_to}))

    barrier = pltpu.get_barrier_semaphore()
    for peer in peers1:
        pl.semaphore_signal(barrier, inc=1, device_id=peer[-1], device_id_type=pl.DeviceIdType.MESH)
    for peer in peers2:
        pl.semaphore_signal(barrier, inc=1, device_id=peer[-1], device_id_type=pl.DeviceIdType.MESH)

    def fetch(b):
        return pltpu.make_async_copy(x_hbm.at[b], xbuf.at[b], in_sem.at[b])

    for b in range(BEAMS):
        fetch(b).start()

    zeros = jnp.zeros((PAD, LANES), jnp.float32)
    for ref, count in ((g, 8), (t5, 16), (t6, 16), (t8, 16), (t9, 16), (t11, 16), (t12, 16)):
        for row in range(count):
            ref[pl.ds(row * PITCH, PAD), :] = zeros
    for row in range(16):
        t13[pl.ds(row * TOP_PITCH, PAD), :] = zeros
        t13[pl.ds(row * TOP_PITCH + PAD, PAD), :] = zeros

    def clear(b, _):
        for row in range(16):
            r1[b, row // 2, row % 2, 0:PAD, :] = zeros
            r2[b, row, 0:PAD, :] = zeros
        return 0

    lax.fori_loop(0, BEAMS, clear, 0)

    block = rev3(j)
    fill_tables(
        spans, shifts, band * 32 + sub, band * 32 + y * 8, block, block * 16 + rev2(y) * 4 + rev2(band)
    )
    to_scalar = pltpu.make_async_copy(shifts, table, table_sem)
    to_scalar.start()
    to_scalar.wait()

    def shift_of(level, entry):
        return table[0, (level - 8) * 16 + entry] if level >= 8 else table[1, (level - 5) * 16 + entry]

    lane = lax.broadcasted_iota(jnp.int32, (BODY, LANES), 1)

    def moved(near, far, amount):
        return pltpu.roll(jnp.where(lane < LANES - amount, near, far), amount, 1)

    def flat(ref):
        def load(row, back):
            return ref[pl.ds(row * PITCH + PAD - back, BODY), :]
        return load

    def flat_store(ref):
        def store(row, value):
            ref[pl.ds(row * PITCH + PAD, BODY), :] = value
        return store

    def small_level(level, rows, load, store, single=False):
        for entry in range(16):
            pair, i = entry // rows, entry % rows
            if single:
                low, high = 2 * pair, 2 * pair + 1
            else:
                low = pair * rows + i // 2
                high = low + rows // 2
            amount = shift_of(level, entry)
            store(entry, load(low, 0) + moved(load(high, 0), load(high, 1), amount))

    def large_level(level, rows, load, store):
        for entry in range(16):
            pair, i = entry // rows, entry % rows
            low = pair * rows + i // 2
            high = low + rows // 2
            shift = shift_of(level, entry)
            whole, amount = jnp.clip(shift // LANES, 0, 2 ** (level - 10) - 1), shift % LANES
            store(entry, load(low, 0) + moved(load(high, whole), load(high, whole + 1), amount))

    member = lax.broadcasted_iota(jnp.int32, (16, 128), 0)
    channel = lax.broadcasted_iota(jnp.int32, (16, 128), 1)
    ones = (channel // 16 == member).astype(jnp.float32).astype(jnp.bfloat16)

    def send_one(b, k):
        to, device = peers1[k]
        return pltpu.make_async_remote_copy(
            src_ref=p7.at[b, pl.ds(2 * rev3(to), 2)],
            dst_ref=r1.at[b, j, :, pl.ds(PAD, BODY), :],
            send_sem=send1.at[b, k],
            recv_sem=recv1.at[b, j],
            device_id=device,
            device_id_type=pl.DeviceIdType.MESH,
        )

    def keep_one(b):
        return pltpu.make_async_copy(
            p7.at[b, pl.ds(2 * rev3(j), 2)], r1.at[b, j, :, pl.ds(PAD, BODY), :], own1.at[b]
        )

    def send_two(b, k):
        y_to, band_to, device = peers2[k]
        return pltpu.make_async_remote_copy(
            src_ref=p10.at[b, rev2(y_to) * 4 + rev2(band_to)],
            dst_ref=r2.at[b, m, pl.ds(PAD, BODY), :],
            send_sem=send2.at[b, k],
            recv_sem=recv2.at[b, m],
            device_id=device,
            device_id_type=pl.DeviceIdType.MESH,
        )

    def keep_two(b):
        return pltpu.make_async_copy(
            p10.at[b, rev2(y) * 4 + rev2(band)], r2.at[b, m, pl.ds(PAD, BODY), :], own2.at[b]
        )

    def first(b):
        fetch(b).wait()

        for c in range(8192 // COLUMNS):
            part = jnp.dot(
                ones, xbuf[b, :, c * COLUMNS : (c + 1) * COLUMNS], preferred_element_type=jnp.float32
            )
            for k in range(COLUMNS // LANES):
                g[pl.ds(PAD + c * (COLUMNS // LANES) + k, 8, stride=PITCH), :] = part[
                    0:8, k * LANES : (k + 1) * LANES
                ]
        small_level(5, 4, flat(g), flat_store(t5), single=True)
        small_level(6, 8, flat(t5), flat_store(t6))

        def keep(row, value):
            p7[b, row] = value

        small_level(7, 16, flat(t6), keep)

    def start_one(b):
        for k in range(len(peers1)):
            send_one(b, k).start()
        keep_one(b).start()

    first(0)
    pl.semaphore_wait(barrier, len(peers1) + len(peers2))
    start_one(0)

    def step_one(b, _):
        first(b)
        start_one(b)
        return 0

    lax.fori_loop(1, BEAMS, step_one, 0)

    def step_two(b, _):
        keep_one(b).wait()
        for to, _ in peers1:
            pltpu.make_async_copy(
                r1.at[b, to, :, pl.ds(PAD, BODY), :], r1.at[b, to, :, pl.ds(PAD, BODY), :], recv1.at[b, to]
            ).wait()

        def load(row, back):
            return r1[b, row // 2, row % 2, PAD - back : PAD - back + BODY, :]

        small_level(8, 4, load, flat_store(t8))
        small_level(9, 8, flat(t8), flat_store(t9))

        def keep(row, value):
            p10[b, row] = value

        small_level(10, 16, flat(t9), keep)
        for k in range(len(peers2)):
            send_two(b, k).start()
        keep_two(b).start()
        return 0

    lax.fori_loop(0, BEAMS, step_two, 0)

    one_lane = lax.broadcasted_iota(jnp.int32, (8, LANES), 1)

    def step_three(b, _):
        keep_two(b).wait()
        for y_to, band_to, _ in peers2:
            n = band_to * 4 + y_to
            pltpu.make_async_copy(
                r2.at[b, n, pl.ds(PAD, BODY), :], r2.at[b, n, pl.ds(PAD, BODY), :], recv2.at[b, n]
            ).wait()
        for entry in range(16):
            pair = entry // 2
            shift = shift_of(11, entry)
            whole, amount = shift // LANES, shift % LANES
            back0 = r2[b, 2 * pair + 1, PAD : PAD + BODY, :]
            back1 = r2[b, 2 * pair + 1, PAD - 1 : PAD - 1 + BODY, :]
            back2 = r2[b, 2 * pair + 1, PAD - 2 : PAD - 2 + BODY, :]
            near = jnp.where(whole == 0, back0, back1)
            far = jnp.where(whole == 0, back1, back2)
            t11[pl.ds(entry * PITCH + PAD, BODY), :] = r2[b, 2 * pair, PAD : PAD + BODY, :] + moved(
                near, far, amount
            )
        large_level(12, 4, flat(t11), flat_store(t12))

        def store13(row, value):
            t13[pl.ds(row * TOP_PITCH + TOP_PAD, BODY), :] = value

        def load13(row, back):
            return t13[pl.ds(row * TOP_PITCH + TOP_PAD - back, BODY), :]

        large_level(13, 8, flat(t12), store13)

        def store14(row, value):
            top[pl.ds(row * BODY, BODY), :] = value * (1.0 / 128.0)

        large_level(14, 16, load13, store14)

        blank = jnp.zeros((8, LANES), jnp.float32)
        for half in range(2):
            rows = slice(half * 8, half * 8 + 8)
            running = [top[pl.ds(half * 8 * BODY + c, 8, stride=BODY), :] for c in range(BODY)]
            for c in range(BODY):
                ded[b, rows, c * LANES : (c + 1) * LANES] = running[c]
            best = running
            for k in range(BOXES - 1):
                width = 2**k
                late = [blank] + running[:-1]
                if width < LANES:
                    late = [
                        pltpu.roll(jnp.where(one_lane < LANES - width, now, old), width, 1)
                        for now, old in zip(running, late)
                    ]
                running = [now + old for now, old in zip(running, late)]
                scale = 1.0 / math.sqrt(2 * width)
                best = [jnp.maximum(high, now * scale) for high, now in zip(best, running)]
            for c in range(BODY):
                peak[b, rows, c * LANES : (c + 1) * LANES] = best[c]
        return 0

    lax.fori_loop(0, BEAMS, step_three, 0)

    def finish(b, _):
        for k in range(len(peers1)):
            send_one(b, k).wait_send()
        for k in range(len(peers2)):
            send_two(b, k).wait_send()
        return 0

    lax.fori_loop(0, BEAMS, finish, 0)


def on_device(intensity, channel_spans):
    plane = jax.ShapeDtypeStruct((BEAMS, ROWS, 8192), jnp.float32)
    vmem = lambda *shape: pltpu.VMEM(shape, jnp.float32)
    dma = pltpu.SemaphoreType.DMA
    return pl.pallas_call(
        kernel,
        out_shape=(plane, plane),
        in_specs=[pl.BlockSpec(memory_space=pltpu.VMEM), pl.BlockSpec(memory_space=pl.ANY)],
        out_specs=(pl.BlockSpec(memory_space=pltpu.VMEM), pl.BlockSpec(memory_space=pltpu.VMEM)),
        scratch_shapes=[
            pltpu.VMEM((8, LANES), jnp.int32),
            pltpu.SMEM((8, LANES), jnp.int32),
            pltpu.VMEM((BEAMS, 128, 8192), jnp.bfloat16),
            vmem(8 * PITCH, LANES),
            vmem(16 * PITCH, LANES),
            vmem(16 * PITCH, LANES),
            vmem(BEAMS, 16, BODY, LANES),
            vmem(BEAMS, 8, 2, PITCH, LANES),
            vmem(16 * PITCH, LANES),
            vmem(16 * PITCH, LANES),
            vmem(BEAMS, 16, BODY, LANES),
            vmem(BEAMS, 16, PITCH, LANES),
            vmem(16 * PITCH, LANES),
            vmem(16 * PITCH, LANES),
            vmem(16 * TOP_PITCH, LANES),
            vmem(16 * BODY, LANES),
            dma,
            dma((BEAMS,)),
            dma((BEAMS, 7)),
            dma((BEAMS, 8)),
            dma((BEAMS,)),
            dma((BEAMS, 15)),
            dma((BEAMS, 16)),
            dma((BEAMS,)),
        ],
        compiler_params=pltpu.CompilerParams(
            collective_id=0, has_side_effects=True, vmem_limit_bytes=48 * 2**20
        ),
    )(channel_spans.reshape(128, LANES), intensity)


def solution(mesh):
    return jax.shard_map(
        on_device,
        mesh=mesh,
        in_specs=(P(None, ("band", "sub"), None), P()),
        out_specs=(P(None, ("band", "sub"), None), P(None, ("band", "sub"), None)),
        check_vma=False,
    )
```

```python
import math

import jax
import jax.numpy as jnp
from jax import lax
from jax.experimental import pallas as pl
from jax.experimental.pallas import tpu as pltpu
from jax.sharding import PartitionSpec as P

ROWS = 16
BOXES = 9
BEAMS = 4
LAST = BEAMS - 1
LANES = 128
BODY = 64
PAD = 8
PITCH = PAD + BODY
TOP_PAD = 16
TOP_PITCH = TOP_PAD + BODY
COLUMNS = 1024


def rev2(v):
    return v % 2 * 2 + v // 2


def rev3(v):
    return v % 2 * 4 + v // 2 % 2 * 2 + v // 4


def powers(index, first):
    value = jnp.full(index.shape, first, jnp.int32)
    for k in range(1, 7):
        value = jnp.where(index == k, first * 2**k, value)
    return value


def quotient(top, bottom):
    guess = (top.astype(jnp.float32) / bottom.astype(jnp.float32)).astype(jnp.int32)
    left = top - guess * bottom
    return jnp.where(left < 0, guess - 1, jnp.where(left >= bottom, guess + 1, guess))


def fill_tables(spans, out, device, group, block, own):
    spread = spans[...].astype(jnp.float32)
    totals = jnp.sum(spread, axis=1, keepdims=True)
    entry = lax.broadcasted_iota(jnp.int32, (1, LANES), 1)
    level = entry // 16
    near = level < 3
    rows = jnp.where(near, powers(level, 4), powers(level - 3, 2))
    half = powers(level, 1)
    start = jnp.where(near, group, 0) + entry % 16 // rows * 2 * half
    r = rows * jnp.where(near, block, own) + entry % 16 % rows
    place = lax.broadcasted_iota(jnp.int32, (128, LANES), 0) - start
    low = jnp.sum(jnp.where((place >= 0) & (place < half), totals, 0.0), axis=0, keepdims=True)
    both = jnp.sum(jnp.where((place >= 0) & (place < 2 * half), totals, 0.0), axis=0, keepdims=True)
    low, both = low.astype(jnp.int32), jnp.maximum(both.astype(jnp.int32), 1)
    out[0:1, :] = quotient(r * low, both)

    mine = spans[pl.ds(device, 1), :].astype(jnp.float32)
    entry = lax.broadcasted_iota(jnp.int32, (48, 1), 0)
    level = entry // 16
    rows = powers(level, 4)
    half = powers(level, 16)
    start = entry % 16 // rows * 2 * half
    r = entry % 16 % rows
    place = lax.broadcasted_iota(jnp.int32, (48, LANES), 1) - start
    low = jnp.sum(jnp.where((place >= 0) & (place < half), mine, 0.0), axis=1, keepdims=True)
    both = jnp.sum(jnp.where((place >= 0) & (place < 2 * half), mine, 0.0), axis=1, keepdims=True)
    low, both = low.astype(jnp.int32), jnp.maximum(both.astype(jnp.int32), 1)
    shifts = quotient(r * low, both).astype(jnp.float32)
    diagonal = entry == lax.broadcasted_iota(jnp.int32, (48, LANES), 1)
    out[1:2, :] = jnp.sum(jnp.where(diagonal, shifts, 0.0), axis=0, keepdims=True).astype(jnp.int32)


def boxcar(top, ded, peak, b, halves=(0, 1)):
    one_lane = lax.broadcasted_iota(jnp.int32, (8, LANES), 1)
    blank = jnp.zeros((8, LANES), jnp.float32)
    for half in halves:
        rows = slice(half * 8, half * 8 + 8)
        running = [top[pl.ds(half * 8 * BODY + c, 8, stride=BODY), :] for c in range(BODY)]
        for c in range(BODY):
            ded[b, rows, c * LANES : (c + 1) * LANES] = running[c]
        best = running
        for k in range(BOXES - 1):
            width = 2**k
            late = [blank] + running[:-1]
            if width < LANES:
                late = [
                    pltpu.roll(jnp.where(one_lane < LANES - width, now, old), width, 1)
                    for now, old in zip(running, late)
                ]
            running = [now + old for now, old in zip(running, late)]
            scale = 1.0 / math.sqrt(2 * width)
            best = [jnp.maximum(high, now * scale) for high, now in zip(best, running)]
        for c in range(BODY):
            peak[b, rows, c * LANES : (c + 1) * LANES] = best[c]


def kernel(
    spans_hbm, x_hbm, ded, peak, top,
    shifts, table, xbuf, g, t5, t6, p7, r1, t8, t9, p10, r2, t11, t12, t13, spans,
    spans_sem, table_sem, in_sem, send1, recv1, own1, send2, recv2, own2,
):
    sub, band = lax.axis_index("sub"), lax.axis_index("band")
    y, z, x_lo = sub // 8, sub // 2 % 4, sub % 2
    x_hi, core = band // 2, band % 2
    j = sub % 8
    m = band * 4 + y

    peers1 = []
    for dz in (0, 1, 3, 2):
        for dx in range(2):
            if dz or dx:
                to = (z + dz) % 4 * 2 + (x_lo + dx) % 2
                peers1.append((to, {"sub": y * 8 + to, "band": band}))
    peers2 = []
    for dy in (0, 1, 3, 2):
        for dh in range(2):
            for dc in range(2):
                if dy or dh or dc:
                    y_to = (y + dy) % 4
                    band_to = (x_hi + dh) % 2 * 2 + (core + dc) % 2
                    peers2.append((y_to, band_to, {"sub": y_to * 8 + j, "band": band_to}))

    barrier = pltpu.get_barrier_semaphore()
    for peer in peers1:
        pl.semaphore_signal(barrier, inc=1, device_id=peer[-1], device_id_type=pl.DeviceIdType.MESH)
    for peer in peers2:
        pl.semaphore_signal(barrier, inc=1, device_id=peer[-1], device_id_type=pl.DeviceIdType.MESH)

    def fetch(b):
        return pltpu.make_async_copy(x_hbm.at[b], xbuf.at[b], in_sem.at[b])

    fetch_spans = pltpu.make_async_copy(spans_hbm, spans, spans_sem)
    fetch_spans.start()
    fetch(0).start()

    zeros = jnp.zeros((PAD, LANES), jnp.float32)
    def clear_rows(*filled):
        for ref, count in filled:
            for row in range(count):
                ref[pl.ds(row * PITCH, PAD), :] = zeros

    clear_rows((g, 8), (t5, 16), (t6, 16))

    block = rev3(j)
    fetch_spans.wait()
    fill_tables(
        spans, shifts, band * 32 + sub, band * 32 + y * 8, block, block * 16 + rev2(y) * 4 + rev2(band)
    )
    to_scalar = pltpu.make_async_copy(shifts, table, table_sem)
    to_scalar.start()
    to_scalar.wait()

    def shift_of(level, entry):
        return table[0, (level - 8) * 16 + entry] if level >= 8 else table[1, (level - 5) * 16 + entry]

    lane = lax.broadcasted_iota(jnp.int32, (BODY, LANES), 1)

    def moved(near, far, amount):
        return pltpu.roll(jnp.where(lane < LANES - amount, near, far), amount, 1)

    def flat(ref):
        def load(row, back):
            return ref[pl.ds(row * PITCH + PAD - back, BODY), :]
        return load

    def flat_store(ref):
        def store(row, value):
            ref[pl.ds(row * PITCH + PAD, BODY), :] = value
        return store

    def small_level(level, rows, load, store, single=False):
        for entry in range(16):
            pair, i = entry // rows, entry % rows
            if single:
                low, high = 2 * pair, 2 * pair + 1
            else:
                low = pair * rows + i // 2
                high = low + rows // 2
            amount = shift_of(level, entry)
            store(entry, load(low, 0) + moved(load(high, 0), load(high, 1), amount))

    def large_level(level, rows, load, store):
        for entry in range(16):
            pair, i = entry // rows, entry % rows
            low = pair * rows + i // 2
            high = low + rows // 2
            shift = shift_of(level, entry)
            whole, amount = jnp.clip(shift // LANES, 0, 2 ** (level - 10) - 1), shift % LANES
            store(entry, load(low, 0) + moved(load(high, whole), load(high, whole + 1), amount))

    member = lax.broadcasted_iota(jnp.int32, (16, 128), 0)
    channel = lax.broadcasted_iota(jnp.int32, (16, 128), 1)
    ones = (channel // 16 == member).astype(jnp.float32).astype(jnp.bfloat16)

    def send_one(b, k):
        to, device = peers1[k]
        return pltpu.make_async_remote_copy(
            src_ref=p7.at[b, pl.ds(2 * rev3(to), 2)],
            dst_ref=r1.at[b, j, :, pl.ds(PAD, BODY), :],
            send_sem=send1.at[b, k],
            recv_sem=recv1.at[b, j],
            device_id=device,
            device_id_type=pl.DeviceIdType.MESH,
        )

    def keep_one(b):
        return pltpu.make_async_copy(
            p7.at[b, pl.ds(2 * rev3(j), 2)], r1.at[b, j, :, pl.ds(PAD, BODY), :], own1.at[b]
        )

    def send_two(b, k):
        y_to, band_to, device = peers2[k]
        return pltpu.make_async_remote_copy(
            src_ref=p10.at[b, rev2(y_to) * 4 + rev2(band_to)],
            dst_ref=r2.at[b, m, pl.ds(PAD, BODY), :],
            send_sem=send2.at[b, k],
            recv_sem=recv2.at[b, m],
            device_id=device,
            device_id_type=pl.DeviceIdType.MESH,
        )

    def keep_two(b):
        return pltpu.make_async_copy(
            p10.at[b, rev2(y) * 4 + rev2(band)], r2.at[b, m, pl.ds(PAD, BODY), :], own2.at[b]
        )

    def first(b):
        for c in range(8192 // COLUMNS):
            part = jnp.dot(
                ones, xbuf[b, :, c * COLUMNS : (c + 1) * COLUMNS], preferred_element_type=jnp.float32
            )
            for k in range(COLUMNS // LANES):
                g[pl.ds(PAD + c * (COLUMNS // LANES) + k, 8, stride=PITCH), :] = part[
                    0:8, k * LANES : (k + 1) * LANES
                ]
        small_level(5, 4, flat(g), flat_store(t5), single=True)
        small_level(6, 8, flat(t5), flat_store(t6))

        def keep(row, value):
            p7[b, row] = value

        small_level(7, 16, flat(t6), keep)

    def start_one(b):
        for k in range(len(peers1)):
            send_one(b, k).start()
        keep_one(b).start()

    fetch(0).wait()
    for b in range(1, BEAMS):
        fetch(b).start()
    first(0)
    pl.semaphore_wait(barrier, len(peers1) + len(peers2))
    start_one(0)

    clear_rows((t8, 16), (t9, 16), (t11, 16), (t12, 16))
    for row in range(16):
        t13[pl.ds(row * TOP_PITCH, PAD), :] = zeros
        t13[pl.ds(row * TOP_PITCH + PAD, PAD), :] = zeros

    def clear(b, _):
        for row in range(16):
            r1[b, row // 2, row % 2, 0:PAD, :] = zeros
            r2[b, row, 0:PAD, :] = zeros
        return 0

    lax.fori_loop(0, BEAMS, clear, 0)

    def step_one(b, _):
        fetch(b).wait()
        first(b)
        start_one(b)
        return 0

    lax.fori_loop(1, BEAMS, step_one, 0)

    def step_two(b, _):
        keep_one(b).wait()
        for to, _ in peers1:
            pltpu.make_async_copy(
                r1.at[b, to, :, pl.ds(PAD, BODY), :], r1.at[b, to, :, pl.ds(PAD, BODY), :], recv1.at[b, to]
            ).wait()

        def load(row, back):
            return r1[b, row // 2, row % 2, PAD - back : PAD - back + BODY, :]

        small_level(8, 4, load, flat_store(t8))
        small_level(9, 8, flat(t8), flat_store(t9))

        def keep(row, value):
            p10[b, row] = value

        small_level(10, 16, flat(t9), keep)
        for k in range(len(peers2)):
            send_two(b, k).start()
        keep_two(b).start()
        return 0

    lax.fori_loop(0, BEAMS, step_two, 0)

    def step_three(b, _):
        keep_two(b).wait()
        for y_to, band_to, _ in peers2:
            n = band_to * 4 + y_to
            pltpu.make_async_copy(
                r2.at[b, n, pl.ds(PAD, BODY), :], r2.at[b, n, pl.ds(PAD, BODY), :], recv2.at[b, n]
            ).wait()
        for entry in range(16):
            pair = entry // 2
            shift = shift_of(11, entry)
            whole, amount = shift // LANES, shift % LANES
            back0 = r2[b, 2 * pair + 1, PAD : PAD + BODY, :]
            back1 = r2[b, 2 * pair + 1, PAD - 1 : PAD - 1 + BODY, :]
            back2 = r2[b, 2 * pair + 1, PAD - 2 : PAD - 2 + BODY, :]
            near = jnp.where(whole == 0, back0, back1)
            far = jnp.where(whole == 0, back1, back2)
            t11[pl.ds(entry * PITCH + PAD, BODY), :] = r2[b, 2 * pair, PAD : PAD + BODY, :] + moved(
                near, far, amount
            )
        large_level(12, 4, flat(t11), flat_store(t12))

        def store13(row, value):
            t13[pl.ds(row * TOP_PITCH + TOP_PAD, BODY), :] = value

        def load13(row, back):
            return t13[pl.ds(row * TOP_PITCH + TOP_PAD - back, BODY), :]

        large_level(13, 8, flat(t12), store13)

        def store14(row, value):
            top[pl.ds(row * BODY, BODY), :] = value * (1.0 / 128.0)

        large_level(14, 16, load13, store14)


        @pl.when(b < LAST)
        def _():
            boxcar(top, ded, peak, b)

        return 0

    lax.fori_loop(0, BEAMS, step_three, 0)

    def finish(b, _):
        for k in range(len(peers1)):
            send_one(b, k).wait_send()
        for k in range(len(peers2)):
            send_two(b, k).wait_send()
        return 0

    lax.fori_loop(0, BEAMS, finish, 0)


def writer(ded_done, peak_done, top, ded, peak, ded_last, peak_last, sem, last_sem):
    copies = []
    for k, (done, out) in enumerate(((ded_done, ded), (peak_done, peak))):
        for b in range(LAST):
            copies.append(pltpu.make_async_copy(done.at[b], out.at[b], sem.at[k, b]))
    for copy in copies:
        copy.start()
    for half in range(2):
        boxcar(top, ded_last, peak_last, 0, (half,))
        rows = pl.ds(8 * half, 8)
        for k, (made, out) in enumerate(((ded_last, ded), (peak_last, peak))):
            copies.append(pltpu.make_async_copy(made.at[0, rows], out.at[LAST, rows], last_sem.at[k, half]))
            copies[-1].start()
    for copy in copies:
        copy.wait()


def on_device(intensity, channel_spans):
    done = jax.ShapeDtypeStruct((LAST, ROWS, 8192), jnp.float32)
    plane = jax.ShapeDtypeStruct((BEAMS, ROWS, 8192), jnp.float32)
    vmem = lambda *shape: pltpu.VMEM(shape, jnp.float32)
    dma = pltpu.SemaphoreType.DMA
    in_vmem = pl.BlockSpec(memory_space=pltpu.VMEM)
    anywhere = pl.BlockSpec(memory_space=pl.ANY)
    ded_done, peak_done, top = pl.pallas_call(
        kernel,
        out_shape=(done, done, jax.ShapeDtypeStruct((16 * BODY, LANES), jnp.float32)),
        in_specs=[anywhere, anywhere],
        out_specs=(in_vmem, in_vmem, in_vmem),
        scratch_shapes=[
            pltpu.VMEM((8, LANES), jnp.int32),
            pltpu.SMEM((8, LANES), jnp.int32),
            pltpu.VMEM((BEAMS, 128, 8192), jnp.bfloat16),
            vmem(8 * PITCH, LANES),
            vmem(16 * PITCH, LANES),
            vmem(16 * PITCH, LANES),
            vmem(BEAMS, 16, BODY, LANES),
            vmem(BEAMS, 8, 2, PITCH, LANES),
            vmem(16 * PITCH, LANES),
            vmem(16 * PITCH, LANES),
            vmem(BEAMS, 16, BODY, LANES),
            vmem(BEAMS, 16, PITCH, LANES),
            vmem(16 * PITCH, LANES),
            vmem(16 * PITCH, LANES),
            vmem(16 * TOP_PITCH, LANES),
            pltpu.VMEM((128, LANES), jnp.int32),
            dma,
            dma,
            dma((BEAMS,)),
            dma((BEAMS, 7)),
            dma((BEAMS, 8)),
            dma((BEAMS,)),
            dma((BEAMS, 15)),
            dma((BEAMS, 16)),
            dma((BEAMS,)),
        ],
        compiler_params=pltpu.CompilerParams(
            collective_id=0, has_side_effects=True, vmem_limit_bytes=48 * 2**20
        ),
    )(channel_spans.reshape(128, LANES), intensity)
    return pl.pallas_call(
        writer,
        out_shape=(plane, plane),
        in_specs=[in_vmem] * 3,
        out_specs=(anywhere, anywhere),
        scratch_shapes=[vmem(1, ROWS, 8192), vmem(1, ROWS, 8192), dma((2, LAST)), dma((2, 2))],
        compiler_params=pltpu.CompilerParams(vmem_limit_bytes=16 * 2**20),
    )(ded_done, peak_done, top)


def solution(mesh):
    return jax.shard_map(
        on_device,
        mesh=mesh,
        in_specs=(P(None, ("band", "sub"), None), P()),
        out_specs=(P(None, ("band", "sub"), None), P(None, ("band", "sub"), None)),
        check_vma=False,
    )
```

```python
import math

import jax
import jax.numpy as jnp
from jax import lax
from jax.experimental import pallas as pl
from jax.experimental.pallas import tpu as pltpu
from jax.sharding import PartitionSpec as P

ROWS = 16
BOXES = 9
BEAMS = 4
LAST = BEAMS - 1
LANES = 128
BODY = 64
PAD = 8
PITCH = PAD + BODY
TOP_PAD = 16
TOP_PITCH = TOP_PAD + BODY
COLUMNS = 1024
SHARED = 1
ALONE = BEAMS - SHARED
ORDER = (3, 0, 1, 2)
PLACE = (0, 1, 3, 2)


def rev2(v):
    return v % 2 * 2 + v // 2


def rev3(v):
    return v % 2 * 4 + v // 2 % 2 * 2 + v // 4


def powers(index, first):
    value = jnp.full(index.shape, first, jnp.int32)
    for k in range(1, 7):
        value = jnp.where(index == k, first * 2**k, value)
    return value


def quotient(top, bottom):
    guess = (top.astype(jnp.float32) / bottom.astype(jnp.float32)).astype(jnp.int32)
    left = top - guess * bottom
    return jnp.where(left < 0, guess - 1, jnp.where(left >= bottom, guess + 1, guess))


def fill_tables(spans, out, device, group, near_block, own, pair_block, blocks, turn):
    spread = spans[...].astype(jnp.float32)
    totals = jnp.sum(spread, axis=1, keepdims=True)
    devices = lax.broadcasted_iota(jnp.int32, (128, LANES), 0)
    entry = lax.broadcasted_iota(jnp.int32, (1, LANES), 1)

    def shifts_of(r, start, half):
        place = devices - start
        low = jnp.sum(jnp.where((place >= 0) & (place < half), totals, 0.0), axis=0, keepdims=True)
        both = jnp.sum(jnp.where((place >= 0) & (place < 2 * half), totals, 0.0), axis=0, keepdims=True)
        return quotient(r * low.astype(jnp.int32), jnp.maximum(both.astype(jnp.int32), 1))

    level = entry // 16
    near = level < 3
    rows = jnp.where(near, powers(level, 4), powers(level - 3, 2))
    half = powers(level, 1)
    start = jnp.where(near, group, 0) + entry % 16 // rows * 2 * half
    out[0:1, :] = shifts_of(rows * jnp.where(near, near_block, own) + entry % 16 % rows, start, half)

    eight, nine = entry < 32, entry < 64
    kept = (entry + turn) % 2
    row9 = 8 * jnp.where(entry % 32 // 16 == 0, blocks[0], blocks[1]) + entry % 8
    row10 = 16 * jnp.where(kept == 0, blocks[0], blocks[1]) + entry % 16
    r = jnp.where(eight, entry, jnp.where(nine, row9, row10))
    start = jnp.where(eight, pair_block, group + jnp.where(nine, entry % 16 // 8 * 4, 0))
    out[3:4, :] = shifts_of(r, start, jnp.where(eight, 1, jnp.where(nine, 2, 4)))

    entry = lax.broadcasted_iota(jnp.int32, (48, 1), 0)
    level = entry // 16
    rows = powers(level, 4)
    half = powers(level, 16)
    start = entry % 16 // rows * 2 * half
    r = entry % 16 % rows
    place = lax.broadcasted_iota(jnp.int32, (48, LANES), 1) - start
    diagonal = entry == lax.broadcasted_iota(jnp.int32, (48, LANES), 1)
    for at, which in ((1, device), (2, 2 * pair_block + 1 - device)):
        mine = spans[pl.ds(which, 1), :].astype(jnp.float32)
        low = jnp.sum(jnp.where((place >= 0) & (place < half), mine, 0.0), axis=1, keepdims=True)
        both = jnp.sum(jnp.where((place >= 0) & (place < 2 * half), mine, 0.0), axis=1, keepdims=True)
        low, both = low.astype(jnp.int32), jnp.maximum(both.astype(jnp.int32), 1)
        shifts = quotient(r * low, both).astype(jnp.float32)
        out[at : at + 1, :] = jnp.sum(jnp.where(diagonal, shifts, 0.0), axis=0, keepdims=True).astype(jnp.int32)


def boxcar(top, ded, peak, b, halves=(0, 1)):
    one_lane = lax.broadcasted_iota(jnp.int32, (8, LANES), 1)
    blank = jnp.zeros((8, LANES), jnp.float32)
    for half in halves:
        rows = slice(half * 8, half * 8 + 8)
        running = [top[pl.ds(half * 8 * BODY + c, 8, stride=BODY), :] for c in range(BODY)]
        for c in range(BODY):
            ded[b, rows, c * LANES : (c + 1) * LANES] = running[c]
        best = running
        for k in range(BOXES - 1):
            width = 2**k
            late = [blank] + running[:-1]
            if width < LANES:
                late = [
                    pltpu.roll(jnp.where(one_lane < LANES - width, now, old), width, 1)
                    for now, old in zip(running, late)
                ]
            running = [now + old for now, old in zip(running, late)]
            scale = 1.0 / math.sqrt(2 * width)
            best = [jnp.maximum(high, now * scale) for high, now in zip(best, running)]
        for c in range(BODY):
            peak[b, rows, c * LANES : (c + 1) * LANES] = best[c]


def kernel(
    spans, x_hbm, ded, peak, top,
    shifts, table, xbuf, g, t5, t6, p7, r1, t8, t9, p10, r2, t11, t12, t13,
    rg, q7, q8, rz, t9q,
    table_sem, in_sem, send1, recv1, own1, send2, recv2, own2, send_x, recv_x, send_z, recv_z, own_z,
):
    sub, band = lax.axis_index("sub"), lax.axis_index("band")
    y, z, x_lo = sub // 8, sub // 2 % 4, sub % 2
    x_hi, core = band // 2, band % 2
    j = sub % 8
    m = band * 4 + y

    peers1, peers_z = [], []
    for dz in (0, 1, 3, 2):
        for dx in range(2):
            z_to = (z + dz) % 4
            to = z_to * 2 + (x_lo + dx) % 2
            device = {"sub": y * 8 + to, "band": band}
            if dz or dx:
                peers1.append((to, device))
            if dz and not dx:
                peers_z.append((z_to, device))
    x_partner = peers1[0][1]
    peers2, peers3 = [], []
    for dy in (0, 1, 3, 2):
        for dh in range(2):
            for dc in range(2):
                if dy or dh or dc:
                    y_to = (y + dy) % 4
                    band_to = (x_hi + dh) % 2 * 2 + (core + dc) % 2
                    peers2.append((y_to, band_to, {"sub": y_to * 8 + j, "band": band_to}))
                    other = y_to * 8 + z * 2 + (x_lo + dh) % 2
                    peers3.append((y_to, band_to, {"sub": other, "band": band_to}, dh))

    barrier = pltpu.get_barrier_semaphore()
    greeted = [p[1] for p in peers1] + [p[2] for p in peers2] + [p[2] for p in peers3 if p[3]]
    for peer in greeted:
        pl.semaphore_signal(barrier, inc=1, device_id=peer, device_id_type=pl.DeviceIdType.MESH)

    def fetch(b):
        return pltpu.make_async_copy(x_hbm.at[PLACE[b]], xbuf.at[b], in_sem.at[b])

    for b in ORDER:
        fetch(b).start()

    zeros = jnp.zeros((PAD, LANES), jnp.float32)
    for ref, count in ((t5, 16), (t6, 16), (t8, 16), (t9, 16), (t11, 16), (t12, 16), (t9q, 32)):
        for row in range(count):
            ref[pl.ds(row * PITCH, PAD), :] = zeros
    for row in range(16):
        t13[pl.ds(row * TOP_PITCH, PAD), :] = zeros
        t13[pl.ds(row * TOP_PITCH + PAD, PAD), :] = zeros

    def clear(b, _):
        for row in range(16):
            r2[b, row, 0:PAD, :] = zeros
        return 0

    lax.fori_loop(0, BEAMS, clear, 0)

    def clear_alone(t, _):
        for row in range(16):
            r1[t, row // 2, row % 2, 0:PAD, :] = zeros
        return 0

    lax.fori_loop(0, ALONE, clear_alone, 0)

    def clear_shared(t, _):
        for row in range(16):
            q7[t, 0, row, 0:PAD, :] = zeros
            q7[t, 1, row, 0:PAD, :] = zeros
        for row in range(32):
            rz[t, row // 8, row // 4 % 2, row % 4, 0:PAD, :] = zeros
        return 0

    lax.fori_loop(0, SHARED, clear_shared, 0)

    block = rev3(j)
    turn = x_lo + x_hi
    device = band * 32 + sub
    fill_tables(
        spans, shifts, device, band * 32 + y * 8, block, block * 16 + rev2(y) * 4 + rev2(band),
        device // 2 * 2, (rev2(z), 4 + rev2(z)), turn,
    )
    to_scalar = pltpu.make_async_copy(shifts, table, table_sem)
    to_scalar.start()
    to_scalar.wait()

    def shift_of(level, entry, at=1):
        return table[0, (level - 8) * 16 + entry] if level >= 8 else table[at, (level - 5) * 16 + entry]

    lane = lax.broadcasted_iota(jnp.int32, (BODY, LANES), 1)

    def moved(near, far, amount):
        return pltpu.roll(jnp.where(lane < LANES - amount, near, far), amount, 1)

    def flat(ref):
        def load(row, back):
            return ref[pl.ds(row * PITCH + PAD - back, BODY), :]
        return load

    def flat_store(ref):
        def store(row, value):
            ref[pl.ds(row * PITCH + PAD, BODY), :] = value
        return store

    top_row = lax.broadcasted_iota(jnp.int32, (BODY, LANES), 0) == 0

    def sums_of(ref, at):
        def load(row, back):
            value = ref[at, pl.ds(row * BODY - back, BODY), :]
            return jnp.where(top_row, 0.0, value) if back else value
        return load

    def small_level(level, rows, load, store, single=False, at=1):
        for entry in range(16):
            pair, i = entry // rows, entry % rows
            if single:
                low, high = 2 * pair, 2 * pair + 1
            else:
                low = pair * rows + i // 2
                high = low + rows // 2
            amount = shift_of(level, entry, at)
            store(entry, load(low, 0) + moved(load(high, 0), load(high, 1), amount))

    def large_level(level, rows, load, store):
        for entry in range(16):
            pair, i = entry // rows, entry % rows
            low = pair * rows + i // 2
            high = low + rows // 2
            shift = shift_of(level, entry)
            whole, amount = jnp.clip(shift // LANES, 0, 2 ** (level - 10) - 1), shift % LANES
            store(entry, load(low, 0) + moved(load(high, whole), load(high, whole + 1), amount))

    member = lax.broadcasted_iota(jnp.int32, (16, 128), 0)
    channel = lax.broadcasted_iota(jnp.int32, (16, 128), 1)
    ones = (channel // 16 == member).astype(jnp.float32).astype(jnp.bfloat16)

    def send_one(b, k):
        to, device = peers1[k]
        return pltpu.make_async_remote_copy(
            src_ref=p7.at[b, pl.ds(2 * rev3(to), 2)],
            dst_ref=r1.at[b, j, :, pl.ds(PAD, BODY), :],
            send_sem=send1.at[b, k],
            recv_sem=recv1.at[b, j],
            device_id=device,
            device_id_type=pl.DeviceIdType.MESH,
        )

    def keep_one(b):
        return pltpu.make_async_copy(
            p7.at[b, pl.ds(2 * rev3(j), 2)], r1.at[b, j, :, pl.ds(PAD, BODY), :], own1.at[b]
        )

    def send_two(b, k):
        y_to, band_to, device = peers2[k]
        return pltpu.make_async_remote_copy(
            src_ref=p10.at[b, rev2(y_to) * 4 + rev2(band_to)],
            dst_ref=r2.at[b, m, pl.ds(PAD, BODY), :],
            send_sem=send2.at[b, k],
            recv_sem=recv2.at[b, m],
            device_id=device,
            device_id_type=pl.DeviceIdType.MESH,
        )

    def keep_two(b):
        return pltpu.make_async_copy(
            p10.at[b, rev2(y) * 4 + rev2(band)], r2.at[b, m, pl.ds(PAD, BODY), :], own2.at[b]
        )

    def send_three(b, k):
        y_to, band_to, device, _ = peers3[k]
        return pltpu.make_async_remote_copy(
            src_ref=p10.at[b, rev2(y_to) * 4 + rev2(band_to)],
            dst_ref=r2.at[b, m, pl.ds(PAD, BODY), :],
            send_sem=send2.at[b, k],
            recv_sem=recv2.at[b, m],
            device_id=device,
            device_id_type=pl.DeviceIdType.MESH,
        )

    def share(t):
        return pltpu.make_async_remote_copy(
            src_ref=g.at[t + ALONE],
            dst_ref=rg.at[t],
            send_sem=send_x.at[t],
            recv_sem=recv_x.at[t],
            device_id=x_partner,
            device_id_type=pl.DeviceIdType.MESH,
        )

    def send_rows(t, k):
        z_to, device = peers_z[k]
        return pltpu.make_async_remote_copy(
            src_ref=q8.at[t, :, pl.ds(4 * rev2(z_to), 4)],
            dst_ref=rz.at[t, z, :, :, pl.ds(PAD, BODY), :],
            send_sem=send_z.at[t, k],
            recv_sem=recv_z.at[t, z],
            device_id=device,
            device_id_type=pl.DeviceIdType.MESH,
        )

    def keep_rows(t):
        return pltpu.make_async_copy(
            q8.at[t, :, pl.ds(4 * rev2(z), 4)], rz.at[t, z, :, :, pl.ds(PAD, BODY), :], own_z.at[t]
        )

    def channel_sums(b):
        fetch(b).wait()
        for c in range(8192 // COLUMNS):
            part = jnp.dot(
                ones, xbuf[b, :, c * COLUMNS : (c + 1) * COLUMNS], preferred_element_type=jnp.float32
            )
            for k in range(COLUMNS // LANES):
                g[b, pl.ds(c * (COLUMNS // LANES) + k, 8, stride=BODY), :] = part[
                    0:8, k * LANES : (k + 1) * LANES
                ]

    def device_rows(load, store, at=1):
        small_level(5, 4, load, flat_store(t5), single=True, at=at)
        small_level(6, 8, flat(t5), flat_store(t6), at=at)
        small_level(7, 16, flat(t6), store, at=at)

    def start_one(b):
        def keep(row, value):
            p7[b, row] = value

        device_rows(sums_of(g, b), keep)
        if b < 2:
            for k in straight:
                send_one(b, k).start()
        keep_one(b).start()

    straight, crossing = (1, 3, 5), (0, 2, 4, 6)

    def start_crossing(b):
        for k in crossing if b < 2 else crossing + straight:
            send_one(b, k).start()

    def pair_rows(t, x, load, at):
        def keep(row, value):
            q7[t, x, row, PAD : PAD + BODY, :] = value

        device_rows(load, keep, at)

    channel_sums(3)
    pl.semaphore_wait(barrier, len(greeted))
    share(0).start()
    channel_sums(0)
    start_one(0)
    start_crossing(0)
    pair_rows(0, x_lo, sums_of(g, 3), 1)
    for b in (1, 2):
        channel_sums(b)
        start_one(b)

    def send_pair_rows(t):
        for k in range(len(peers_z)):
            send_rows(t, k).start()
        keep_rows(t).start()

    def step_pair(t):
        pair_rows(t, 1 - x_lo, sums_of(rg, t), 2)
        for r in range(32):
            near = q7[t, 1, r // 2, PAD : PAD + BODY, :]
            far = q7[t, 1, r // 2, PAD - 1 : PAD - 1 + BODY, :]
            q8[t, r // 16, r % 16] = q7[t, 0, r // 2, PAD : PAD + BODY, :] + moved(near, far, table[3, r])

    share(0).wait_recv()
    start_crossing(1)
    step_pair(0)
    send_pair_rows(0)

    def wait_ring(t):
        keep_rows(t).wait()
        for z_to, _ in peers_z:
            pltpu.make_async_copy(
                rz.at[t, z_to, :, :, pl.ds(PAD, BODY), :], rz.at[t, z_to, :, :, pl.ds(PAD, BODY), :],
                recv_z.at[t, z_to],
            ).wait()

    def wait_one(b):
        keep_one(b).wait()
        for to, _ in peers1:
            pltpu.make_async_copy(
                r1.at[b, to, :, pl.ds(PAD, BODY), :], r1.at[b, to, :, pl.ds(PAD, BODY), :], recv1.at[b, to]
            ).wait()

    def step_two(b):
        def load(row, back):
            return r1[b, row // 2, row % 2, PAD - back : PAD - back + BODY, :]

        small_level(8, 4, load, flat_store(t8))
        small_level(9, 8, flat(t8), flat_store(t9))

        def keep(row, value):
            p10[b, row] = value

        small_level(10, 16, flat(t9), keep)
        for k in range(len(peers2)):
            send_two(b, k).start()
        keep_two(b).start()

    def step_ring(t):
        for entry in range(32):
            side, pair, i = entry // 16, entry // 8 % 2, entry % 8
            near = rz[t, 2 * pair + 1, side, i // 2, PAD : PAD + BODY, :]
            far = rz[t, 2 * pair + 1, side, i // 2, PAD - 1 : PAD - 1 + BODY, :]
            t9q[pl.ds(entry * PITCH + PAD, BODY), :] = rz[
                t, 2 * pair, side, i // 2, PAD : PAD + BODY, :
            ] + moved(near, far, table[3, 32 + entry])
        for row in range(16):
            low = (turn + row) % 2 * 16 + row // 2

            def load(at, back):
                start = pl.multiple_of(at * PITCH, 8) + (PAD - back)
                return t9q[pl.ds(start, BODY), :]

            p10[t + ALONE, row] = load(low, 0) + moved(load(low + 8, 0), load(low + 8, 1), table[3, 64 + row])
        for k in range(len(peers3)):
            send_three(t + ALONE, k).start()
        keep_two(t + ALONE).start()

    def step_three(b):
        keep_two(b).wait()
        for y_to, band_to, _ in peers2:
            n = band_to * 4 + y_to
            pltpu.make_async_copy(
                r2.at[b, n, pl.ds(PAD, BODY), :], r2.at[b, n, pl.ds(PAD, BODY), :], recv2.at[b, n]
            ).wait()
        for entry in range(16):
            pair = entry // 2
            shift = shift_of(11, entry)
            whole, amount = shift // LANES, shift % LANES
            back0 = r2[b, 2 * pair + 1, PAD : PAD + BODY, :]
            back1 = r2[b, 2 * pair + 1, PAD - 1 : PAD - 1 + BODY, :]
            back2 = r2[b, 2 * pair + 1, PAD - 2 : PAD - 2 + BODY, :]
            near = jnp.where(whole == 0, back0, back1)
            far = jnp.where(whole == 0, back1, back2)
            t11[pl.ds(entry * PITCH + PAD, BODY), :] = r2[b, 2 * pair, PAD : PAD + BODY, :] + moved(
                near, far, amount
            )
        large_level(12, 4, flat(t11), flat_store(t12))

        def store13(row, value):
            t13[pl.ds(row * TOP_PITCH + TOP_PAD, BODY), :] = value

        def load13(row, back):
            return t13[pl.ds(row * TOP_PITCH + TOP_PAD - back, BODY), :]

        large_level(13, 8, flat(t12), store13)

        def store14(row, value):
            top[pl.ds(row * BODY, BODY), :] = value * (1.0 / 128.0)

        large_level(14, 16, load13, store14)

        if PLACE[b] < LAST:
            boxcar(top, ded, peak, PLACE[b])

    wait_one(0)
    step_two(0)
    wait_one(1)
    start_crossing(2)
    step_two(1)
    wait_ring(0)
    step_ring(0)
    wait_one(2)
    step_two(2)
    step_three(0)
    step_three(1)
    step_three(3)
    step_three(2)

    def finish_alone(t, _):
        for k in range(len(peers1)):
            send_one(t, k).wait_send()
        for k in range(len(peers2)):
            send_two(t, k).wait_send()
        return 0

    lax.fori_loop(0, ALONE, finish_alone, 0)

    def finish_shared(t, _):
        share(t).wait_send()
        for k in range(len(peers_z)):
            send_rows(t, k).wait_send()
        for k in range(len(peers3)):
            send_three(t + ALONE, k).wait_send()
        return 0

    lax.fori_loop(0, SHARED, finish_shared, 0)


def writer(ded_done, peak_done, top, ded, peak, ded_last, peak_last, sem, last_sem):
    copies = []
    for k, (done, out) in enumerate(((ded_done, ded), (peak_done, peak))):
        for b in range(LAST):
            copies.append(pltpu.make_async_copy(done.at[b], out.at[b], sem.at[k, b]))
    for copy in copies:
        copy.start()
    for half in range(2):
        boxcar(top, ded_last, peak_last, 0, (half,))
        rows = pl.ds(8 * half, 8)
        for k, (made, out) in enumerate(((ded_last, ded), (peak_last, peak))):
            copies.append(pltpu.make_async_copy(made.at[0, rows], out.at[LAST, rows], last_sem.at[k, half]))
            copies[-1].start()
    for copy in copies:
        copy.wait()


def on_device(intensity, channel_spans):
    done = jax.ShapeDtypeStruct((LAST, ROWS, 8192), jnp.float32)
    plane = jax.ShapeDtypeStruct((BEAMS, ROWS, 8192), jnp.float32)
    vmem = lambda *shape: pltpu.VMEM(shape, jnp.float32)
    dma = pltpu.SemaphoreType.DMA
    in_vmem = pl.BlockSpec(memory_space=pltpu.VMEM)
    anywhere = pl.BlockSpec(memory_space=pl.ANY)
    ded_done, peak_done, top = pl.pallas_call(
        kernel,
        out_shape=(done, done, jax.ShapeDtypeStruct((16 * BODY, LANES), jnp.float32)),
        in_specs=[in_vmem, anywhere],
        out_specs=(in_vmem, in_vmem, in_vmem),
        scratch_shapes=[
            pltpu.VMEM((8, LANES), jnp.int32),
            pltpu.SMEM((8, LANES), jnp.int32),
            pltpu.VMEM((BEAMS, 128, 8192), jnp.bfloat16),
            vmem(BEAMS, 8 * BODY, LANES),
            vmem(16 * PITCH, LANES),
            vmem(16 * PITCH, LANES),
            vmem(ALONE, 16, BODY, LANES),
            vmem(ALONE, 8, 2, PITCH, LANES),
            vmem(16 * PITCH, LANES),
            vmem(16 * PITCH, LANES),
            vmem(BEAMS, 16, BODY, LANES),
            vmem(BEAMS, 16, PITCH, LANES),
            vmem(16 * PITCH, LANES),
            vmem(16 * PITCH, LANES),
            vmem(16 * TOP_PITCH, LANES),
            vmem(SHARED, 8 * BODY, LANES),
            vmem(SHARED, 2, 16, PITCH, LANES),
            vmem(SHARED, 2, 16, BODY, LANES),
            vmem(SHARED, 4, 2, 4, PITCH, LANES),
            vmem(32 * PITCH, LANES),
            dma,
            dma((BEAMS,)),
            dma((ALONE, 7)),
            dma((ALONE, 8)),
            dma((ALONE,)),
            dma((BEAMS, 15)),
            dma((BEAMS, 16)),
            dma((BEAMS,)),
            dma((SHARED,)),
            dma((SHARED,)),
            dma((SHARED, 3)),
            dma((SHARED, 4)),
            dma((SHARED,)),
        ],
        compiler_params=pltpu.CompilerParams(
            collective_id=0, has_side_effects=True, vmem_limit_bytes=48 * 2**20
        ),
    )(channel_spans.reshape(128, LANES), intensity)
    return pl.pallas_call(
        writer,
        out_shape=(plane, plane),
        in_specs=[in_vmem] * 3,
        out_specs=(anywhere, anywhere),
        scratch_shapes=[vmem(1, ROWS, 8192), vmem(1, ROWS, 8192), dma((2, LAST)), dma((2, 2))],
        compiler_params=pltpu.CompilerParams(vmem_limit_bytes=16 * 2**20),
    )(ded_done, peak_done, top)


def solution(mesh):
    return jax.shard_map(
        on_device,
        mesh=mesh,
        in_specs=(P(None, ("band", "sub"), None), P()),
        out_specs=(P(None, ("band", "sub"), None), P(None, ("band", "sub"), None)),
        check_vma=False,
    )
```

```python
import math

import jax
import jax.numpy as jnp
from jax import lax
from jax.experimental import pallas as pl
from jax.experimental.pallas import tpu as pltpu
from jax.sharding import PartitionSpec as P

ROWS = 16
BOXES = 9
BEAMS = 4
LAST = BEAMS - 1
LANES = 128
BODY = 64
PAD = 8
PITCH = PAD + BODY
TOP_PAD = 16
TOP_PITCH = TOP_PAD + BODY
COLUMNS = 1024
SHARED = 1
ALONE = BEAMS - SHARED
ORDER = (3, 0, 1, 2)
PLACE = (0, 1, 3, 2)


def rev2(v):
    return v % 2 * 2 + v // 2


def rev3(v):
    return v % 2 * 4 + v // 2 % 2 * 2 + v // 4


def powers(index, first):
    value = jnp.full(index.shape, first, jnp.int32)
    for k in range(1, 7):
        value = jnp.where(index == k, first * 2**k, value)
    return value


def quotient(top, bottom):
    guess = (top.astype(jnp.float32) / bottom.astype(jnp.float32)).astype(jnp.int32)
    left = top - guess * bottom
    return jnp.where(left < 0, guess - 1, jnp.where(left >= bottom, guess + 1, guess))


def fill_tables(spans, out, device, group, near_block, own, pair_block, blocks, turn):
    spread = spans[...].astype(jnp.float32)
    totals = jnp.sum(spread, axis=1, keepdims=True)
    devices = lax.broadcasted_iota(jnp.int32, (128, LANES), 0)
    entry = lax.broadcasted_iota(jnp.int32, (1, LANES), 1)

    def shifts_of(r, start, half):
        place = devices - start
        low = jnp.sum(jnp.where((place >= 0) & (place < half), totals, 0.0), axis=0, keepdims=True)
        both = jnp.sum(jnp.where((place >= 0) & (place < 2 * half), totals, 0.0), axis=0, keepdims=True)
        return quotient(r * low.astype(jnp.int32), jnp.maximum(both.astype(jnp.int32), 1))

    level = entry // 16
    near = level < 3
    rows = jnp.where(near, powers(level, 4), powers(level - 3, 2))
    half = powers(level, 1)
    start = jnp.where(near, group, 0) + entry % 16 // rows * 2 * half
    out[0:1, :] = shifts_of(rows * jnp.where(near, near_block, own) + entry % 16 % rows, start, half)

    eight, nine = entry < 32, entry < 64
    kept = (entry + turn) % 2
    row9 = 8 * jnp.where(entry % 32 // 16 == 0, blocks[0], blocks[1]) + entry % 8
    row10 = 16 * jnp.where(kept == 0, blocks[0], blocks[1]) + entry % 16
    r = jnp.where(eight, entry, jnp.where(nine, row9, row10))
    start = jnp.where(eight, pair_block, group + jnp.where(nine, entry % 16 // 8 * 4, 0))
    out[3:4, :] = shifts_of(r, start, jnp.where(eight, 1, jnp.where(nine, 2, 4)))

    entry = lax.broadcasted_iota(jnp.int32, (48, 1), 0)
    level = entry // 16
    rows = powers(level, 4)
    half = powers(level, 16)
    start = entry % 16 // rows * 2 * half
    r = entry % 16 % rows
    place = lax.broadcasted_iota(jnp.int32, (48, LANES), 1) - start
    diagonal = entry == lax.broadcasted_iota(jnp.int32, (48, LANES), 1)
    for at, which in ((1, device), (2, 2 * pair_block + 1 - device)):
        mine = spans[pl.ds(which, 1), :].astype(jnp.float32)
        low = jnp.sum(jnp.where((place >= 0) & (place < half), mine, 0.0), axis=1, keepdims=True)
        both = jnp.sum(jnp.where((place >= 0) & (place < 2 * half), mine, 0.0), axis=1, keepdims=True)
        low, both = low.astype(jnp.int32), jnp.maximum(both.astype(jnp.int32), 1)
        shifts = quotient(r * low, both).astype(jnp.float32)
        out[at : at + 1, :] = jnp.sum(jnp.where(diagonal, shifts, 0.0), axis=0, keepdims=True).astype(jnp.int32)


def boxcar(top, ded, peak, b, halves=(0, 1)):
    one_lane = lax.broadcasted_iota(jnp.int32, (8, LANES), 1)
    blank = jnp.zeros((8, LANES), jnp.float32)
    for half in halves:
        rows = slice(half * 8, half * 8 + 8)
        running = [top[pl.ds(half * 8 * BODY + c, 8, stride=BODY), :] for c in range(BODY)]
        for c in range(BODY):
            ded[b, rows, c * LANES : (c + 1) * LANES] = running[c]
        best = running
        for k in range(BOXES - 1):
            width = 2**k
            late = [blank] + running[:-1]
            if width < LANES:
                late = [
                    pltpu.roll(jnp.where(one_lane < LANES - width, now, old), width, 1)
                    for now, old in zip(running, late)
                ]
            running = [now + old for now, old in zip(running, late)]
            scale = 1.0 / math.sqrt(2 * width)
            best = [jnp.maximum(high, now * scale) for high, now in zip(best, running)]
        for c in range(BODY):
            peak[b, rows, c * LANES : (c + 1) * LANES] = best[c]


def kernel(
    spans, x_hbm, ded, peak, top,
    shifts, table, xbuf, g, t5, t6, p7, r1, t8, t9, p10, r2, t11, t12, t13,
    rg, q7, q8, rz, t9q,
    table_sem, in_sem, send1, recv1, own1, send2, recv2, own2, send_x, recv_x, send_z, recv_z, own_z,
):
    sub, band = lax.axis_index("sub"), lax.axis_index("band")
    y, z, x_lo = sub // 8, sub // 2 % 4, sub % 2
    x_hi, core = band // 2, band % 2
    j = sub % 8
    m = band * 4 + y

    peers1, peers_z = [], []
    for dz in (0, 1, 3, 2):
        for dx in range(2):
            z_to = (z + dz) % 4
            to = z_to * 2 + (x_lo + dx) % 2
            device = {"sub": y * 8 + to, "band": band}
            if dz or dx:
                peers1.append((to, device))
            if dz and not dx:
                peers_z.append((z_to, device))
    x_partner = peers1[0][1]
    peers2, peers3 = [], []
    for dy in (0, 1, 3, 2):
        for dh in range(2):
            for dc in range(2):
                if dy or dh or dc:
                    y_to = (y + dy) % 4
                    band_to = (x_hi + dh) % 2 * 2 + (core + dc) % 2
                    peers2.append((y_to, band_to, {"sub": y_to * 8 + j, "band": band_to}))
                    other = y_to * 8 + z * 2 + (x_lo + dh) % 2
                    peers3.append((y_to, band_to, {"sub": other, "band": band_to}, dh))

    barrier = pltpu.get_barrier_semaphore()
    greeted = [p[1] for p in peers1] + [p[2] for p in peers2] + [p[2] for p in peers3 if p[3]]
    for peer in greeted:
        pl.semaphore_signal(barrier, inc=1, device_id=peer, device_id_type=pl.DeviceIdType.MESH)

    def fetch(b):
        return pltpu.make_async_copy(x_hbm.at[PLACE[b]], xbuf.at[b], in_sem.at[b])

    fetch(ORDER[0]).start()

    zeros = jnp.zeros((PAD, LANES), jnp.float32)
    for row in range(16):
        t5[pl.ds(row * PITCH, PAD), :] = zeros
        t6[pl.ds(row * PITCH, PAD), :] = zeros

    block = rev3(j)
    turn = x_lo + x_hi
    device = band * 32 + sub
    fill_tables(
        spans, shifts, device, band * 32 + y * 8, block, block * 16 + rev2(y) * 4 + rev2(band),
        device // 2 * 2, (rev2(z), 4 + rev2(z)), turn,
    )
    to_scalar = pltpu.make_async_copy(shifts, table, table_sem)
    to_scalar.start()
    to_scalar.wait()

    def shift_of(level, entry, at=1):
        return table[0, (level - 8) * 16 + entry] if level >= 8 else table[at, (level - 5) * 16 + entry]

    lane = lax.broadcasted_iota(jnp.int32, (BODY, LANES), 1)

    def moved(near, far, amount):
        return pltpu.roll(jnp.where(lane < LANES - amount, near, far), amount, 1)

    def flat(ref):
        def load(row, back):
            return ref[pl.ds(row * PITCH + PAD - back, BODY), :]
        return load

    def flat_store(ref):
        def store(row, value):
            ref[pl.ds(row * PITCH + PAD, BODY), :] = value
        return store

    top_row = lax.broadcasted_iota(jnp.int32, (BODY, LANES), 0) == 0

    def sums_of(ref, at):
        def load(row, back):
            value = ref[at, pl.ds(row * BODY - back, BODY), :]
            return jnp.where(top_row, 0.0, value) if back else value
        return load

    def small_level(level, rows, load, store, single=False, at=1):
        for entry in range(16):
            pair, i = entry // rows, entry % rows
            if single:
                low, high = 2 * pair, 2 * pair + 1
            else:
                low = pair * rows + i // 2
                high = low + rows // 2
            amount = shift_of(level, entry, at)
            store(entry, load(low, 0) + moved(load(high, 0), load(high, 1), amount))

    def large_level(level, rows, load, store):
        for entry in range(16):
            pair, i = entry // rows, entry % rows
            low = pair * rows + i // 2
            high = low + rows // 2
            shift = shift_of(level, entry)
            whole, amount = jnp.clip(shift // LANES, 0, 2 ** (level - 10) - 1), shift % LANES
            store(entry, load(low, 0) + moved(load(high, whole), load(high, whole + 1), amount))

    member = lax.broadcasted_iota(jnp.int32, (16, 128), 0)
    channel = lax.broadcasted_iota(jnp.int32, (16, 128), 1)
    ones = (channel // 16 == member).astype(jnp.float32).astype(jnp.bfloat16)

    def send_one(b, k):
        to, device = peers1[k]
        return pltpu.make_async_remote_copy(
            src_ref=p7.at[b, pl.ds(2 * rev3(to), 2)],
            dst_ref=r1.at[b, j, :, pl.ds(PAD, BODY), :],
            send_sem=send1.at[b, k],
            recv_sem=recv1.at[b, j],
            device_id=device,
            device_id_type=pl.DeviceIdType.MESH,
        )

    def keep_one(b):
        return pltpu.make_async_copy(
            p7.at[b, pl.ds(2 * rev3(j), 2)], r1.at[b, j, :, pl.ds(PAD, BODY), :], own1.at[b]
        )

    def send_two(b, k):
        y_to, band_to, device = peers2[k]
        return pltpu.make_async_remote_copy(
            src_ref=p10.at[b, rev2(y_to) * 4 + rev2(band_to)],
            dst_ref=r2.at[b, m, pl.ds(PAD, BODY), :],
            send_sem=send2.at[b, k],
            recv_sem=recv2.at[b, m],
            device_id=device,
            device_id_type=pl.DeviceIdType.MESH,
        )

    def keep_two(b):
        return pltpu.make_async_copy(
            p10.at[b, rev2(y) * 4 + rev2(band)], r2.at[b, m, pl.ds(PAD, BODY), :], own2.at[b]
        )

    def send_three(b, k):
        y_to, band_to, device, _ = peers3[k]
        return pltpu.make_async_remote_copy(
            src_ref=p10.at[b, rev2(y_to) * 4 + rev2(band_to)],
            dst_ref=r2.at[b, m, pl.ds(PAD, BODY), :],
            send_sem=send2.at[b, k],
            recv_sem=recv2.at[b, m],
            device_id=device,
            device_id_type=pl.DeviceIdType.MESH,
        )

    def share(t):
        return pltpu.make_async_remote_copy(
            src_ref=g.at[t + ALONE],
            dst_ref=rg.at[t],
            send_sem=send_x.at[t],
            recv_sem=recv_x.at[t],
            device_id=x_partner,
            device_id_type=pl.DeviceIdType.MESH,
        )

    def send_rows(t, k):
        z_to, device = peers_z[k]
        return pltpu.make_async_remote_copy(
            src_ref=q8.at[t, :, pl.ds(4 * rev2(z_to), 4)],
            dst_ref=rz.at[t, z, :, :, pl.ds(PAD, BODY), :],
            send_sem=send_z.at[t, k],
            recv_sem=recv_z.at[t, z],
            device_id=device,
            device_id_type=pl.DeviceIdType.MESH,
        )

    def keep_rows(t):
        return pltpu.make_async_copy(
            q8.at[t, :, pl.ds(4 * rev2(z), 4)], rz.at[t, z, :, :, pl.ds(PAD, BODY), :], own_z.at[t]
        )

    def channel_sums(b):
        fetch(b).wait()
        if b == ORDER[0]:
            for later in ORDER[1:]:
                fetch(later).start()
        for c in range(8192 // COLUMNS):
            part = jnp.dot(
                ones, xbuf[b, :, c * COLUMNS : (c + 1) * COLUMNS], preferred_element_type=jnp.float32
            )
            for k in range(COLUMNS // LANES):
                g[b, pl.ds(c * (COLUMNS // LANES) + k, 8, stride=BODY), :] = part[
                    0:8, k * LANES : (k + 1) * LANES
                ]

    def device_rows(load, store, at=1):
        small_level(5, 4, load, flat_store(t5), single=True, at=at)
        small_level(6, 8, flat(t5), flat_store(t6), at=at)
        small_level(7, 16, flat(t6), store, at=at)

    def start_one(b):
        def keep(row, value):
            p7[b, row] = value

        device_rows(sums_of(g, b), keep)
        if b < 2:
            for k in straight:
                send_one(b, k).start()
        keep_one(b).start()

    straight, crossing = (1, 3, 5), (0, 2, 4, 6)

    def start_crossing(b):
        for k in crossing if b < 2 else crossing + straight:
            send_one(b, k).start()

    def pair_rows(t, x, load, at):
        def keep(row, value):
            q7[t, x, row, PAD : PAD + BODY, :] = value

        device_rows(load, keep, at)

    channel_sums(3)
    pl.semaphore_wait(barrier, len(greeted))
    share(0).start()
    channel_sums(0)
    start_one(0)
    start_crossing(0)
    for ref, count in ((t8, 16), (t9, 16), (t11, 16), (t12, 16), (t9q, 32)):
        for row in range(count):
            ref[pl.ds(row * PITCH, PAD), :] = zeros
    for row in range(16):
        t13[pl.ds(row * TOP_PITCH, PAD), :] = zeros
        t13[pl.ds(row * TOP_PITCH + PAD, PAD), :] = zeros

    def clear(b, _):
        for row in range(16):
            r2[b, row, 0:PAD, :] = zeros
        return 0

    lax.fori_loop(0, BEAMS, clear, 0)

    def clear_alone(t, _):
        for row in range(16):
            r1[t, row // 2, row % 2, 0:PAD, :] = zeros
        return 0

    lax.fori_loop(0, ALONE, clear_alone, 0)

    def clear_shared(t, _):
        for row in range(16):
            q7[t, 0, row, 0:PAD, :] = zeros
            q7[t, 1, row, 0:PAD, :] = zeros
        for row in range(32):
            rz[t, row // 8, row // 4 % 2, row % 4, 0:PAD, :] = zeros
        return 0

    lax.fori_loop(0, SHARED, clear_shared, 0)
    pair_rows(0, x_lo, sums_of(g, 3), 1)
    for b in (1, 2):
        channel_sums(b)
        start_one(b)

    def send_pair_rows(t):
        for k in range(len(peers_z)):
            send_rows(t, k).start()
        keep_rows(t).start()

    def step_pair(t):
        pair_rows(t, 1 - x_lo, sums_of(rg, t), 2)
        for r in range(32):
            near = q7[t, 1, r // 2, PAD : PAD + BODY, :]
            far = q7[t, 1, r // 2, PAD - 1 : PAD - 1 + BODY, :]
            q8[t, r // 16, r % 16] = q7[t, 0, r // 2, PAD : PAD + BODY, :] + moved(near, far, table[3, r])

    share(0).wait_recv()
    start_crossing(1)
    step_pair(0)
    send_pair_rows(0)

    def wait_ring(t):
        keep_rows(t).wait()
        for z_to, _ in peers_z:
            pltpu.make_async_copy(
                rz.at[t, z_to, :, :, pl.ds(PAD, BODY), :], rz.at[t, z_to, :, :, pl.ds(PAD, BODY), :],
                recv_z.at[t, z_to],
            ).wait()

    def wait_one(b):
        keep_one(b).wait()
        for to, _ in peers1:
            pltpu.make_async_copy(
                r1.at[b, to, :, pl.ds(PAD, BODY), :], r1.at[b, to, :, pl.ds(PAD, BODY), :], recv1.at[b, to]
            ).wait()

    def step_two(b):
        def load(row, back):
            return r1[b, row // 2, row % 2, PAD - back : PAD - back + BODY, :]

        small_level(8, 4, load, flat_store(t8))
        small_level(9, 8, flat(t8), flat_store(t9))

        def keep(row, value):
            p10[b, row] = value

        small_level(10, 16, flat(t9), keep)
        for k in range(len(peers2)):
            send_two(b, k).start()
        keep_two(b).start()

    def step_ring(t):
        for entry in range(32):
            side, pair, i = entry // 16, entry // 8 % 2, entry % 8
            near = rz[t, 2 * pair + 1, side, i // 2, PAD : PAD + BODY, :]
            far = rz[t, 2 * pair + 1, side, i // 2, PAD - 1 : PAD - 1 + BODY, :]
            t9q[pl.ds(entry * PITCH + PAD, BODY), :] = rz[
                t, 2 * pair, side, i // 2, PAD : PAD + BODY, :
            ] + moved(near, far, table[3, 32 + entry])
        for row in range(16):
            low = (turn + row) % 2 * 16 + row // 2

            def load(at, back):
                start = pl.multiple_of(at * PITCH, 8) + (PAD - back)
                return t9q[pl.ds(start, BODY), :]

            p10[t + ALONE, row] = load(low, 0) + moved(load(low + 8, 0), load(low + 8, 1), table[3, 64 + row])
        for k in range(len(peers3)):
            send_three(t + ALONE, k).start()
        keep_two(t + ALONE).start()

    def step_three(b):
        keep_two(b).wait()
        for y_to, band_to, _ in peers2:
            n = band_to * 4 + y_to
            pltpu.make_async_copy(
                r2.at[b, n, pl.ds(PAD, BODY), :], r2.at[b, n, pl.ds(PAD, BODY), :], recv2.at[b, n]
            ).wait()
        for entry in range(16):
            pair = entry // 2
            shift = shift_of(11, entry)
            whole, amount = shift // LANES, shift % LANES
            back0 = r2[b, 2 * pair + 1, PAD : PAD + BODY, :]
            back1 = r2[b, 2 * pair + 1, PAD - 1 : PAD - 1 + BODY, :]
            back2 = r2[b, 2 * pair + 1, PAD - 2 : PAD - 2 + BODY, :]
            near = jnp.where(whole == 0, back0, back1)
            far = jnp.where(whole == 0, back1, back2)
            t11[pl.ds(entry * PITCH + PAD, BODY), :] = r2[b, 2 * pair, PAD : PAD + BODY, :] + moved(
                near, far, amount
            )
        large_level(12, 4, flat(t11), flat_store(t12))

        def store13(row, value):
            t13[pl.ds(row * TOP_PITCH + TOP_PAD, BODY), :] = value

        def load13(row, back):
            return t13[pl.ds(row * TOP_PITCH + TOP_PAD - back, BODY), :]

        large_level(13, 8, flat(t12), store13)

        def store14(row, value):
            top[pl.ds(row * BODY, BODY), :] = value * (1.0 / 128.0)

        large_level(14, 16, load13, store14)

        if PLACE[b] < LAST:
            boxcar(top, ded, peak, PLACE[b])

    wait_one(0)
    step_two(0)
    wait_one(1)
    start_crossing(2)
    step_two(1)
    wait_ring(0)
    step_ring(0)
    wait_one(2)
    step_two(2)
    step_three(0)
    step_three(1)
    step_three(3)
    step_three(2)

    def finish_alone(t, _):
        for k in range(len(peers1)):
            send_one(t, k).wait_send()
        for k in range(len(peers2)):
            send_two(t, k).wait_send()
        return 0

    lax.fori_loop(0, ALONE, finish_alone, 0)

    def finish_shared(t, _):
        share(t).wait_send()
        for k in range(len(peers_z)):
            send_rows(t, k).wait_send()
        for k in range(len(peers3)):
            send_three(t + ALONE, k).wait_send()
        return 0

    lax.fori_loop(0, SHARED, finish_shared, 0)


def writer(ded_done, peak_done, top, ded, peak, ded_last, peak_last, sem, last_sem):
    copies = []
    for k, (done, out) in enumerate(((ded_done, ded), (peak_done, peak))):
        for b in range(LAST):
            copies.append(pltpu.make_async_copy(done.at[b], out.at[b], sem.at[k, b]))
    for copy in copies:
        copy.start()
    for half in range(2):
        boxcar(top, ded_last, peak_last, 0, (half,))
        rows = pl.ds(8 * half, 8)
        for k, (made, out) in enumerate(((ded_last, ded), (peak_last, peak))):
            copies.append(pltpu.make_async_copy(made.at[0, rows], out.at[LAST, rows], last_sem.at[k, half]))
            copies[-1].start()
    for copy in copies:
        copy.wait()


def on_device(intensity, channel_spans):
    done = jax.ShapeDtypeStruct((LAST, ROWS, 8192), jnp.float32)
    plane = jax.ShapeDtypeStruct((BEAMS, ROWS, 8192), jnp.float32)
    vmem = lambda *shape: pltpu.VMEM(shape, jnp.float32)
    dma = pltpu.SemaphoreType.DMA
    in_vmem = pl.BlockSpec(memory_space=pltpu.VMEM)
    anywhere = pl.BlockSpec(memory_space=pl.ANY)
    ded_done, peak_done, top = pl.pallas_call(
        kernel,
        out_shape=(done, done, jax.ShapeDtypeStruct((16 * BODY, LANES), jnp.float32)),
        in_specs=[in_vmem, anywhere],
        out_specs=(in_vmem, in_vmem, in_vmem),
        scratch_shapes=[
            pltpu.VMEM((8, LANES), jnp.int32),
            pltpu.SMEM((8, LANES), jnp.int32),
            pltpu.VMEM((BEAMS, 128, 8192), jnp.bfloat16),
            vmem(BEAMS, 8 * BODY, LANES),
            vmem(16 * PITCH, LANES),
            vmem(16 * PITCH, LANES),
            vmem(ALONE, 16, BODY, LANES),
            vmem(ALONE, 8, 2, PITCH, LANES),
            vmem(16 * PITCH, LANES),
            vmem(16 * PITCH, LANES),
            vmem(BEAMS, 16, BODY, LANES),
            vmem(BEAMS, 16, PITCH, LANES),
            vmem(16 * PITCH, LANES),
            vmem(16 * PITCH, LANES),
            vmem(16 * TOP_PITCH, LANES),
            vmem(SHARED, 8 * BODY, LANES),
            vmem(SHARED, 2, 16, PITCH, LANES),
            vmem(SHARED, 2, 16, BODY, LANES),
            vmem(SHARED, 4, 2, 4, PITCH, LANES),
            vmem(32 * PITCH, LANES),
            dma,
            dma((BEAMS,)),
            dma((ALONE, 7)),
            dma((ALONE, 8)),
            dma((ALONE,)),
            dma((BEAMS, 15)),
            dma((BEAMS, 16)),
            dma((BEAMS,)),
            dma((SHARED,)),
            dma((SHARED,)),
            dma((SHARED, 3)),
            dma((SHARED, 4)),
            dma((SHARED,)),
        ],
        compiler_params=pltpu.CompilerParams(
            collective_id=0, has_side_effects=True, vmem_limit_bytes=48 * 2**20
        ),
    )(channel_spans.reshape(128, LANES), intensity)
    return pl.pallas_call(
        writer,
        out_shape=(plane, plane),
        in_specs=[in_vmem] * 3,
        out_specs=(anywhere, anywhere),
        scratch_shapes=[vmem(1, ROWS, 8192), vmem(1, ROWS, 8192), dma((2, LAST)), dma((2, 2))],
        compiler_params=pltpu.CompilerParams(vmem_limit_bytes=16 * 2**20),
    )(ded_done, peak_done, top)


def solution(mesh):
    return jax.shard_map(
        on_device,
        mesh=mesh,
        in_specs=(P(None, ("band", "sub"), None), P()),
        out_specs=(P(None, ("band", "sub"), None), P(None, ("band", "sub"), None)),
        check_vma=False,
    )
```
